512 devices in a mesh: node: 128 (over y, z, core), col: 4 (over x).
Axes of the slice: x: 4, y: 4, z: 16, core: 2. Of those that a mesh axis runs over, the one named last changes fastest.
Arguments:
- features: bfloat16 [131072, 128], P('node', 'col'), may hold values from -6 to 6
- local_tiles: bfloat16 [1024, 128, 128], P('node'), may hold values from -0.125 to 0.125
- hub_tiles: bfloat16 [1024, 2, 128, 128], P('node'), may hold values from -0.125 to 0.125
- hub_ref: int32 [1024, 2], P('node'), may hold values from 0 to 127
- hub_list: int32 [128], P('node'), may hold values from 0 to 7
- send_list: int32 [128, 128], P('node'), may hold values from 0 to 7
- stripe_tiles: bfloat16 [16384, 128, 128], P('node'), may hold values from -0.125 to 0.125
- stripe_slot: int32 [128, 128], P('node'), may hold values from 0 to 127, as said below
- stripe_target: int32 [128, 128], P('node'), may hold values from 0 to 7
- stripe_live: int32 [128], P('node'), may hold values from 96 to 128, as said below
- weight: bfloat16 [128, 128], replicated, may hold values from -0.5 to 0.5
Outputs:
- layer_out: bfloat16 [131072, 128], P('node', 'col')
The draws below stay inside these ranges and needn't reach their ends.
Inputs may be any that keep to these rules, and one draw needn't show every extreme that they name: `stripe_slot`: each row names every node device exactly once. `stripe_live`: equal to 128 on at least one node device.
All inputs are finite; a program needn't handle non-finite values.
Results may differ from the reference program's by a relative error of at most 0.0049.
Values may be sent and summed in bfloat16 or wider, within the bound.
No kernel may reach another device: no remote copies, remote signals or barrier semaphores. Data moves between devices by JAX's collectives and lax.ppermute only.
A program may use at most 64 MiB of HBM per device.

```python
import jax
import jax.numpy as jnp
from jax import lax

F = 128
TILE = 128
HT = 2
ROWB = 8
CAP = 128
NB = 1024
NODES = 131072
N_NODE = 128


def draw_stripe_slot(key, part):
    key = jax.random.fold_in(key, 11)
    keys = jax.random.split(key, N_NODE)
    rows = jax.vmap(lambda one: jax.random.permutation(one, N_NODE))(keys)
    return rows.astype(jnp.int32)


def draw_stripe_live(key, part):
    key = jax.random.fold_in(key, 7)
    first, second = jax.random.split(key)
    counts = jax.random.randint(first, (N_NODE,), CAP - CAP // 4, CAP + 1)
    fullest = jax.random.randint(second, (), 0, N_NODE)
    marker = jnp.arange(N_NODE, dtype=jnp.int32) == fullest
    return jnp.where(marker, CAP, counts).astype(jnp.int32)


def with_ends(array, own_key, smallest, top_value):
    shape = array.shape
    place = [jax.random.randint(jax.random.fold_in(own_key, axis), (), 0, shape[axis]) for axis in range(len(shape))]
    array = array.at[tuple(place)].set(smallest)
    longest = shape.index(max(shape))
    place[longest] = (place[longest] + 1) % shape[longest]
    return array.at[tuple(place)].set(top_value)


def levels(rng, shape, cuts, low, largest):
    gain = 1.0
    for position, blocks in cuts:
        heights = jax.random.uniform(jax.random.fold_in(jax.random.fold_in(rng, 6), position), (blocks,), jnp.float32, low / len(cuts), largest / len(cuts))
        gain = gain * jnp.repeat(jnp.exp(heights), shape[position] // blocks).reshape((-1,) + (1,) * (len(shape) - 1 - position))
    return gain


def gaussian(rng, dims, spread, most, cuts=(), held_as=jnp.bfloat16):
    drawn = jax.random.normal(rng, dims, jnp.float32) * spread
    if len(cuts) > 0:
        drawn = levels(rng, dims, cuts, -0.22, 0.18) * drawn
    return jnp.clip(drawn, min=-most, max=most).astype(held_as)


def setup_inputs(seed: int = 0) -> dict:
    streams_of = jax.random.split(jax.random.key(seed), 12)
    features = gaussian(streams_of[0], (NODES, F), 1.0, 6.0, ((0, 128), (1, 4)))
    local_tiles = gaussian(streams_of[1], (NB, TILE, TILE), (TILE * (3 + CAP // ROWB)) ** -0.5, 0.125, ((0, 128),))
    hub_tiles = gaussian(streams_of[2], (NB, HT, TILE, TILE), (TILE * (3 + CAP // ROWB)) ** -0.5, 0.125, ((0, 128),))
    hub_ref = with_ends(jax.random.randint(streams_of[3], (NB, HT), 0, N_NODE), jax.random.fold_in(streams_of[3], 1), 0, N_NODE - 1).astype(jnp.int32)
    hub_list = with_ends(jax.random.randint(streams_of[4], (N_NODE,), 0, ROWB), jax.random.fold_in(streams_of[4], 1), 0, ROWB - 1).astype(jnp.int32)
    send_list = with_ends(jax.random.randint(streams_of[5], (N_NODE, N_NODE), 0, ROWB), jax.random.fold_in(streams_of[5], 1), 0, ROWB - 1).astype(jnp.int32)
    stripe_tiles = gaussian(streams_of[6], (N_NODE * CAP, TILE, TILE), (TILE * (3 + CAP // ROWB)) ** -0.5, 0.125, ((0, 128),))
    stripe_slot = draw_stripe_slot(jax.random.fold_in(streams_of[11], 71), 0)
    stripe_target = with_ends(jax.random.randint(streams_of[8], (N_NODE, CAP), 0, ROWB), jax.random.fold_in(streams_of[8], 1), 0, ROWB - 1).astype(jnp.int32)
    stripe_live = draw_stripe_live(jax.random.fold_in(streams_of[11], 71), 0)
    weight = gaussian(streams_of[10], (F, F), F ** -0.5, 0.5)
    return dict(features=features, local_tiles=local_tiles, hub_tiles=hub_tiles, hub_ref=hub_ref, hub_list=hub_list, send_list=send_list, stripe_tiles=stripe_tiles, stripe_slot=stripe_slot, stripe_target=stripe_target, stripe_live=stripe_live, weight=weight)


def reference(features, local_tiles, hub_tiles, hub_ref, hub_list, send_list, stripe_tiles, stripe_slot, stripe_target, stripe_live, weight):
    blocks = features.reshape(NB, TILE, F)
    local_sum = jnp.einsum("btu,buf->btf", local_tiles.astype(jnp.float32), blocks.astype(jnp.float32))
    hub_ids = (jnp.arange(N_NODE, dtype=jnp.int32) * ROWB + hub_list).astype(jnp.int32)
    hub_blocks = blocks[hub_ids]
    picked = hub_blocks[hub_ref]
    hub_sum = jnp.einsum("bjtu,bjuf->btf", hub_tiles.astype(jnp.float32), picked.astype(jnp.float32))

    def device_part(device):
        tiles = lax.dynamic_slice_in_dim(stripe_tiles, (device * CAP).astype(jnp.int32), CAP, 0)
        slots = stripe_slot[device]
        source = (slots * ROWB + send_list[slots, device]).astype(jnp.int32)
        taken = blocks[source]
        prods = jnp.einsum("ctu,cuf->ctf", tiles.astype(jnp.float32), taken.astype(jnp.float32))
        live = jnp.arange(CAP, dtype=jnp.int32) < stripe_live[device]
        onehot = ((stripe_target[device][None, :] == jnp.arange(ROWB, dtype=jnp.int32)[:, None]) & live[None, :]).astype(jnp.float32)
        summed = jnp.dot(onehot, prods.reshape(CAP, TILE * F), precision=lax.Precision.HIGHEST)
        return summed.reshape(ROWB, TILE, F)

    stripe_sum = lax.map(device_part, jnp.arange(N_NODE, dtype=jnp.int32)).reshape(NB, TILE, F)
    aggregated = (local_sum + hub_sum + stripe_sum).astype(jnp.bfloat16).reshape(NODES, F)
    return jnp.dot(aggregated, weight, preferred_element_type=jnp.float32).astype(jnp.bfloat16)
```

```python
import functools

import jax
import jax.numpy as jnp
from jax import lax
from jax.experimental import pallas as pl
from jax.experimental.pallas import tpu as pltpu
from jax.sharding import Mesh, PartitionSpec as P

Y, H, L, C, COL = 4, 4, 4, 2, 4
ROWB, TILE, W = 8, 128, 32
NEAR = Y * L * C
CAP = 128
BLOCKS = ROWB * W
PAY = BLOCKS + 16
CHUNKS = 8
NT = (((1,), (1,)), ((), ()))
VMEM = pl.BlockSpec(memory_space=pltpu.VMEM)
SMEM = pl.BlockSpec(memory_space=pltpu.SMEM)
ANY = pl.BlockSpec(memory_space=pl.ANY)


def rows_of(start):
    return pl.ds(pl.multiple_of(start, 16), W)


def pack_kernel(hub_list, feat, send, out):
    for b in range(ROWB):
        out[b * W : (b + 1) * W, :] = feat[:, b * TILE : (b + 1) * TILE]
    row = lax.broadcasted_iota(jnp.int32, (16, TILE), 0)
    sends = jnp.broadcast_to(send[...], (16, TILE))
    meta = jnp.where(row == 0, sends, hub_list[0])
    out[BLOCKS:PAY, :] = meta.astype(jnp.float32).astype(jnp.bfloat16)


def select_kernel(gathered, out, hubs, index_vmem, index, sem):
    for h in range(H):
        meta = gathered[h * PAY + BLOCKS : (h + 1) * PAY, :].astype(jnp.float32)
        index_vmem[h * 8 : h * 8 + 8, :] = meta[:8].astype(jnp.int32)
    copy = pltpu.make_async_copy(index_vmem, index, sem)
    copy.start()
    copy.wait()
    cube = lax.axis_index("h")
    for h in range(H):
        hubs[h * W : (h + 1) * W, :] = gathered[rows_of(h * PAY + index[h * 8 + 1, 0] * W), :]
    for m in range(NEAR):
        reader = (m // (L * C)) * (H * L * C) + cube * (L * C) + m % (L * C)
        for h in range(H):
            block = index[h * 8, reader]
            at = (m * H + h) * W
            out[at : at + W, :] = gathered[rows_of(h * PAY + block * W), :]


def base_kernel(hub_ref, feat, local_tiles, hub_tiles, hubs_own, hubs_other, out):
    core = lax.axis_index("c")
    for b in range(ROWB):
        total = lax.dot_general(
            feat[:, b * TILE : (b + 1) * TILE], local_tiles[b], NT, preferred_element_type=jnp.float32
        )
        for j in range(2):
            hub = hub_ref[b, j]
            y = lax.shift_right_logical(hub, 5)
            h = lax.shift_right_logical(hub, 3) & 3
            l = lax.shift_right_logical(hub, 1) & 3
            at = rows_of(((y * L + l) * H + h) * W)
            block = jnp.where((hub & 1) == core, hubs_own[at, :], hubs_other[at, :])
            total += lax.dot_general(block, hub_tiles[b, j], NT, preferred_element_type=jnp.float32)
        out[b * W : (b + 1) * W, :] = total


def stripe_kernel(slot, target, live, received, base, tiles_hbm, out, tiles, acc, sems):
    each = CAP // CHUNKS
    copies = []
    for k in range(CHUNKS):
        part = pl.ds(k * each, each)
        copies.append(pltpu.make_async_copy(tiles_hbm.at[part], tiles.at[part], sems.at[k]))
        copies[-1].start()
    acc[0:BLOCKS, :] = base[...]
    acc[BLOCKS:, :] = jnp.zeros((W, TILE), jnp.float32)
    count = live[0]
    for k in range(CHUNKS):
        copies[k].wait()
        for s in range(k * each, (k + 1) * each):
            q = slot[0, s]
            y = lax.shift_right_logical(q, 5)
            h = lax.shift_right_logical(q, 3) & 3
            near = y * (L * C) + (q & 7)
            block = received[rows_of((near * H + h) * W), :]
            prod = lax.dot_general(block, tiles[s], NT, preferred_element_type=jnp.float32)
            row = jnp.where(s < count, target[0, s], ROWB)
            acc[rows_of(row * W), :] += prod
    for b in range(ROWB):
        agg = acc[b * W : (b + 1) * W, :].astype(jnp.bfloat16)
        for k in range(COL):
            out[k * W : (k + 1) * W, b * TILE : (b + 1) * TILE] = agg


def local(
    features,
    local_tiles,
    hub_tiles,
    hub_ref,
    hub_list,
    send_list,
    stripe_tiles,
    stripe_slot,
    stripe_target,
    stripe_live,
    weight,
):
    bf16, f32 = jnp.bfloat16, jnp.float32
    params = pltpu.CompilerParams(vmem_limit_bytes=32 * 1024 * 1024)
    feat = features.T
    payload = pl.pallas_call(
        pack_kernel,
        out_shape=jax.ShapeDtypeStruct((PAY, TILE), bf16),
        in_specs=[SMEM, VMEM, VMEM],
        out_specs=VMEM,
        compiler_params=params,
        name="pack",
    )(hub_list, feat, send_list)
    gathered = lax.all_gather(payload, "h", axis=0, tiled=True)
    outgoing, hubs = pl.pallas_call(
        select_kernel,
        out_shape=(
            jax.ShapeDtypeStruct((NEAR * H * W, TILE), bf16),
            jax.ShapeDtypeStruct((H * W, TILE), bf16),
        ),
        in_specs=[VMEM],
        out_specs=(VMEM, VMEM),
        scratch_shapes=[
            pltpu.VMEM((H * 8, TILE), jnp.int32),
            pltpu.SMEM((H * 8, TILE), jnp.int32),
            pltpu.SemaphoreType.DMA,
        ],
        compiler_params=params,
        name="select",
    )(gathered)
    hubs_l = lax.all_gather(hubs, "l", axis=0, tiled=True)
    hubs_l, outgoing = lax.optimization_barrier((hubs_l, outgoing))
    received = lax.all_to_all(outgoing, ("y", "l", "c"), split_axis=0, concat_axis=0, tiled=True)
    hubs_own = lax.all_gather(hubs_l, "y", axis=0, tiled=True)
    hubs_other = lax.ppermute(hubs_own, "c", [(0, 1), (1, 0)])
    base = pl.pallas_call(
        base_kernel,
        out_shape=jax.ShapeDtypeStruct((BLOCKS, TILE), f32),
        in_specs=[SMEM, VMEM, VMEM, VMEM, VMEM, VMEM],
        out_specs=VMEM,
        compiler_params=params,
        cost_estimate=pl.CostEstimate(flops=25_000_000, bytes_accessed=2_000_000, transcendentals=0),
        name="base",
    )(hub_ref, feat, local_tiles, hub_tiles, hubs_own, hubs_other)
    aggregated = pl.pallas_call(
        stripe_kernel,
        out_shape=jax.ShapeDtypeStruct((COL * W, ROWB * TILE), bf16),
        in_specs=[SMEM, SMEM, SMEM, VMEM, VMEM, ANY],
        out_specs=VMEM,
        scratch_shapes=[
            pltpu.VMEM((CAP, TILE, TILE), bf16),
            pltpu.VMEM((BLOCKS + W, TILE), f32),
            pltpu.SemaphoreType.DMA((CHUNKS,)),
        ],
        compiler_params=params,
        name="stripes",
    )(stripe_slot, stripe_target, stripe_live, received, base, stripe_tiles)
    full = lax.all_to_all(aggregated, "x", split_axis=0, concat_axis=0, tiled=True)
    weight_cols = lax.dynamic_slice_in_dim(weight, lax.axis_index("x") * W, W, 1)
    result = jnp.dot(weight_cols.T, full, preferred_element_type=f32)
    return result.astype(bf16).T


def solution(mesh):
    split = Mesh(mesh.devices.reshape(Y, H, L, C, COL), ("y", "h", "l", "c", "x"))
    node = ("y", "h", "l", "c")
    in_specs = (
        P(node, "x"),
        P(node, None, None),
        P(node, None, None, None),
        P(node, None),
        P(node),
        P(node, None),
        P(node, None, None),
        P(node, None),
        P(node, None),
        P(node),
        P(),
    )
    return jax.shard_map(local, mesh=split, in_specs=in_specs, out_specs=P(node, "x"), check_vma=False)
```

```python
import jax
import jax.numpy as jnp
from jax import lax
from jax.experimental import pallas as pl
from jax.experimental.pallas import tpu as pltpu
from jax.sharding import Mesh, PartitionSpec as P

Y, H, L, C, COL = 4, 8, 2, 2, 4
ROWB, TILE, W = 8, 128, 32
NEAR = Y * L * C
CAP = 128
EARLY = 40
PARTS = 4
BLOCKS = ROWB * W
META = BLOCKS + W
PAY = META + 16
SENT = 2 * H * W
NT = (((1,), (1,)), ((), ()))
VMEM = pl.BlockSpec(memory_space=pltpu.VMEM)
SMEM = pl.BlockSpec(memory_space=pltpu.SMEM)
ANY = pl.BlockSpec(memory_space=pl.ANY)


def rows_of(start):
    return pl.ds(pl.multiple_of(start, 16), W)


def in_hbm(array):
    return pltpu.with_memory_space_constraint(array, pltpu.HBM)


def in_vmem(array):
    return pltpu.with_memory_space_constraint(array, pltpu.VMEM)


def pack_kernel(hub_list, feat, send, out):
    for b in range(ROWB):
        out[b * W : (b + 1) * W, :] = feat[:, b * TILE : (b + 1) * TILE]
    sends = jnp.broadcast_to(send[...], (16, TILE))
    out[META:PAY, :] = sends.astype(jnp.float32).astype(jnp.bfloat16)
    out[BLOCKS:META, :] = out[rows_of(hub_list[0] * W), :]


def select_kernel(gathered, out, index_vmem, index, buffer, sem, sems):
    for h in range(H):
        meta = gathered[h * PAY + META : (h + 1) * PAY, :].astype(jnp.float32)
        index_vmem[h * 8 : h * 8 + 8, :] = meta[:8].astype(jnp.int32)
    copy = pltpu.make_async_copy(index_vmem, index, sem)
    copy.start()
    for m in range(NEAR):
        for h in range(H):
            at = (H + h) * W
            buffer[m, at : at + W, :] = gathered[h * PAY + BLOCKS : h * PAY + META, :]
    copy.wait()
    pair = lax.axis_index("h")
    copies = []
    for m in range(NEAR):
        reader = (m // (L * C)) * (H * L * C) + pair * (L * C) + m % (L * C)
        for h in range(H):
            block = index[h * 8, reader]
            buffer[m, h * W : (h + 1) * W, :] = gathered[rows_of(h * PAY + block * W), :]
        copies.append(pltpu.make_async_copy(buffer.at[m], out.at[m], sems.at[m]))
        copies[-1].start()
    for copy in copies:
        copy.wait()


def fetch_kernel(feat, local_tiles, tiles_hbm, out, tiles, sem):
    copy = pltpu.make_async_copy(tiles_hbm.at[pl.ds(0, EARLY)], tiles, sem)
    copy.start()
    for b in range(ROWB):
        out[b * W : (b + 1) * W, :] = lax.dot_general(
            feat[:, b * TILE : (b + 1) * TILE], local_tiles[b], NT, preferred_element_type=jnp.float32
        )
    copy.wait()


def stripe_kernel(
    hub_ref, slot, target, live, received, base, early, hub_hbm, tiles_hbm, out, hub_tiles, late, acc, hub_sem, sems
):
    each = (CAP - EARLY) // PARTS
    hub_copy = pltpu.make_async_copy(hub_hbm, hub_tiles, hub_sem)
    hub_copy.start()
    copies = []
    for k in range(PARTS):
        source = tiles_hbm.at[pl.ds(EARLY + k * each, each)]
        copies.append(pltpu.make_async_copy(source, late.at[pl.ds(k * each, each)], sems.at[k]))
        copies[-1].start()

    def place(node):
        near = lax.shift_right_logical(node, 5) * (L * C) + (node & 3)
        return near * SENT, (lax.shift_right_logical(node, 2) & 7) * W

    def product(tile, start):
        return lax.dot_general(tile, received[rows_of(start), :], NT, preferred_element_type=jnp.float32)

    for b in range(ROWB + 1):
        acc[b] = jnp.zeros((TILE, W), jnp.float32)
    count = live[0]
    for s in range(CAP):
        if s == EARLY:
            hub_copy.wait()
            for b in range(ROWB):
                total = acc[b]
                for j in range(2):
                    near, at = place(hub_ref[b, j])
                    total += product(hub_tiles[b, j], near + H * W + at)
                acc[b] = total
        if s >= EARLY and (s - EARLY) % each == 0:
            copies[(s - EARLY) // each].wait()
        tile = early[s] if s < EARLY else late[s - EARLY]
        near, at = place(slot[0, s])
        row = jnp.where(s < count, target[0, s], ROWB)
        acc[row] += product(tile, near + at)
    for b in range(ROWB):
        agg = (acc[b].T + base[b * W : (b + 1) * W, :]).astype(jnp.bfloat16)
        for k in range(COL):
            out[k * W : (k + 1) * W, b * TILE : (b + 1) * TILE] = agg


def local(
    features,
    local_tiles,
    hub_tiles,
    hub_ref,
    hub_list,
    send_list,
    stripe_tiles,
    stripe_slot,
    stripe_target,
    stripe_live,
    weight,
):
    bf16, f32 = jnp.bfloat16, jnp.float32
    params = pltpu.CompilerParams(vmem_limit_bytes=16 * 1024 * 1024)
    feat = features.T
    payload = pl.pallas_call(
        pack_kernel,
        out_shape=jax.ShapeDtypeStruct((PAY, TILE), bf16),
        in_specs=[SMEM, VMEM, VMEM],
        out_specs=VMEM,
        compiler_params=params,
        name="pack",
    )(hub_list, in_hbm(feat), in_hbm(send_list))
    gathered = lax.all_gather(payload, "h", axis=0, tiled=True)
    outgoing = pl.pallas_call(
        select_kernel,
        out_shape=jax.ShapeDtypeStruct((NEAR, SENT, TILE), bf16),
        in_specs=[VMEM],
        out_specs=ANY,
        scratch_shapes=[
            pltpu.VMEM((H * 8, TILE), jnp.int32),
            pltpu.SMEM((H * 8, TILE), jnp.int32),
            pltpu.VMEM((NEAR, SENT, TILE), bf16),
            pltpu.SemaphoreType.DMA,
            pltpu.SemaphoreType.DMA((NEAR,)),
        ],
        compiler_params=params,
        cost_estimate=pl.CostEstimate(flops=0, bytes_accessed=6_000_000, transcendentals=0),
        name="select",
    )(gathered)
    outgoing, feat = lax.optimization_barrier((outgoing, feat))
    received = lax.all_to_all(outgoing, ("y", "l", "c"), split_axis=0, concat_axis=0, tiled=True)
    base, early = pl.pallas_call(
        fetch_kernel,
        out_shape=(pltpu.VMEM((BLOCKS, TILE), f32), pltpu.VMEM((EARLY, TILE, TILE), bf16)),
        in_specs=[VMEM, VMEM, ANY],
        out_specs=(VMEM, ANY),
        scratch_shapes=[pltpu.SemaphoreType.DMA],
        compiler_params=params,
        cost_estimate=pl.CostEstimate(flops=8_400_000, bytes_accessed=3_000_000, transcendentals=0),
        name="fetch",
    )(in_hbm(feat), in_hbm(local_tiles), in_hbm(stripe_tiles))
    aggregated = pl.pallas_call(
        stripe_kernel,
        out_shape=jax.ShapeDtypeStruct((COL * W, ROWB * TILE), bf16),
        in_specs=[SMEM, SMEM, SMEM, SMEM, VMEM, VMEM, VMEM, ANY, ANY],
        out_specs=VMEM,
        scratch_shapes=[
            pltpu.VMEM((ROWB, 2, TILE, TILE), bf16),
            pltpu.VMEM((CAP - EARLY, TILE, TILE), bf16),
            pltpu.VMEM((ROWB + 1, TILE, W), f32),
            pltpu.SemaphoreType.DMA,
            pltpu.SemaphoreType.DMA((PARTS,)),
        ],
        compiler_params=params,
        name="stripes",
    )(
        hub_ref,
        stripe_slot,
        stripe_target,
        stripe_live,
        received.reshape(NEAR * SENT, TILE),
        in_vmem(base),
        in_vmem(early),
        in_hbm(hub_tiles),
        in_hbm(stripe_tiles),
    )
    full = lax.all_to_all(aggregated, "x", split_axis=0, concat_axis=0, tiled=True)
    weight_cols = lax.dynamic_slice_in_dim(weight, lax.axis_index("x") * W, W, 1)
    result = jnp.dot(weight_cols.T, full, preferred_element_type=f32)
    return result.astype(bf16).T


def solution(mesh):
    split = Mesh(mesh.devices.reshape(Y, H, L, C, COL), ("y", "h", "l", "c", "x"))
    node = ("y", "h", "l", "c")
    in_specs = (
        P(node, "x"),
        P(node, None, None),
        P(node, None, None, None),
        P(node, None),
        P(node),
        P(node, None),
        P(node, None, None),
        P(node, None),
        P(node, None),
        P(node),
        P(),
    )
    return jax.shard_map(local, mesh=split, in_specs=in_specs, out_specs=P(node, "x"), check_vma=False)
```

```python
import jax
import jax.numpy as jnp
from jax import lax
from jax.experimental import pallas as pl
from jax.experimental.pallas import tpu as pltpu
from jax.sharding import Mesh, PartitionSpec as P

Y, H, L, C, COL = 4, 8, 2, 2, 4
ROWB, TILE, W = 8, 128, 32
NEAR = Y * L * C
CAP = 128
EARLY = 40
PARTS = 4
BLOCKS = ROWB * W
META = BLOCKS + W
PAY = META + 16
SENT = 2 * H * W
NT = (((1,), (1,)), ((), ()))
VMEM = pl.BlockSpec(memory_space=pltpu.VMEM)
SMEM = pl.BlockSpec(memory_space=pltpu.SMEM)
ANY = pl.BlockSpec(memory_space=pl.ANY)


def rows_of(start):
    return pl.ds(pl.multiple_of(start, 16), W)


def in_hbm(array):
    return pltpu.with_memory_space_constraint(array, pltpu.HBM)


def in_vmem(array):
    return pltpu.with_memory_space_constraint(array, pltpu.VMEM)


def pack_kernel(hub_list, feat, send, out):
    for b in range(ROWB):
        out[b * W : (b + 1) * W, :] = feat[:, b * TILE : (b + 1) * TILE]
    sends = jnp.broadcast_to(send[...], (16, TILE))
    out[META:PAY, :] = sends.astype(jnp.float32).astype(jnp.bfloat16)
    out[BLOCKS:META, :] = out[rows_of(hub_list[0] * W), :]


def select_kernel(gathered, out, index_vmem, index, buffer, sem, sems):
    for h in range(H):
        meta = gathered[h * PAY + META : (h + 1) * PAY, :].astype(jnp.float32)
        index_vmem[h : h + 1, :] = meta[:1].astype(jnp.int32)
    copy = pltpu.make_async_copy(index_vmem, index, sem)
    copy.start()
    for m in range(NEAR):
        for h in range(H):
            at = (H + h) * W
            buffer[m, at : at + W, :] = gathered[h * PAY + BLOCKS : h * PAY + META, :]
    copy.wait()
    pair = lax.axis_index("h")
    copies = []
    for m in range(NEAR):
        reader = (m // (L * C)) * (H * L * C) + pair * (L * C) + m % (L * C)
        for h in range(H):
            block = index[h, reader]
            buffer[m, h * W : (h + 1) * W, :] = gathered[rows_of(h * PAY + block * W), :]
        copies.append(pltpu.make_async_copy(buffer.at[m], out.at[m], sems.at[m]))
        copies[-1].start()
    for copy in copies:
        copy.wait()


def fetch_kernel(feat, local_tiles, tiles_hbm, out, tiles, sem):
    copy = pltpu.make_async_copy(tiles_hbm.at[pl.ds(0, EARLY)], tiles, sem)
    copy.start()
    for b in range(ROWB):
        out[b * W : (b + 1) * W, :] = lax.dot_general(
            feat[:, b * TILE : (b + 1) * TILE], local_tiles[b], NT, preferred_element_type=jnp.float32
        )
    copy.wait()


def stripe_kernel(
    hub_ref, slot, target, live, received, base, early, hub_hbm, tiles_hbm, out, hub_tiles, late, acc, hub_sem, sems
):
    each = (CAP - EARLY) // PARTS
    hub_copy = pltpu.make_async_copy(hub_hbm, hub_tiles, hub_sem)
    hub_copy.start()
    copies = []
    for k in range(PARTS):
        source = tiles_hbm.at[pl.ds(EARLY + k * each, each)]
        copies.append(pltpu.make_async_copy(source, late.at[pl.ds(k * each, each)], sems.at[k]))
        copies[-1].start()

    def place(node):
        near = lax.shift_right_logical(node, 5) * (L * C) + (node & 3)
        return near * SENT, (lax.shift_right_logical(node, 2) & 7) * W

    def product(tile, start):
        return lax.dot_general(tile, received[rows_of(start), :], NT, preferred_element_type=jnp.float32)

    for b in range(ROWB + 1):
        acc[b] = jnp.zeros((TILE, W), jnp.float32)
    count = live[0]
    for s in range(CAP):
        if s == EARLY:
            hub_copy.wait()
            for b in range(ROWB):
                total = acc[b]
                for j in range(2):
                    near, at = place(hub_ref[b, j])
                    total += product(hub_tiles[b, j], near + H * W + at)
                acc[b] = total
        if s >= EARLY and (s - EARLY) % each == 0:
            copies[(s - EARLY) // each].wait()
        tile = early[s] if s < EARLY else late[s - EARLY]
        near, at = place(slot[0, s])
        row = jnp.where(s < count, target[0, s], ROWB)
        acc[row] += product(tile, near + at)
    for b in range(ROWB):
        agg = (acc[b].T + base[b * W : (b + 1) * W, :]).astype(jnp.bfloat16)
        for k in range(COL):
            out[k * W : (k + 1) * W, b * TILE : (b + 1) * TILE] = agg


def local(
    features,
    local_tiles,
    hub_tiles,
    hub_ref,
    hub_list,
    send_list,
    stripe_tiles,
    stripe_slot,
    stripe_target,
    stripe_live,
    weight,
):
    bf16, f32 = jnp.bfloat16, jnp.float32
    params = pltpu.CompilerParams(vmem_limit_bytes=16 * 1024 * 1024)
    feat = features.T
    payload = pl.pallas_call(
        pack_kernel,
        out_shape=jax.ShapeDtypeStruct((PAY, TILE), bf16),
        in_specs=[SMEM, VMEM, VMEM],
        out_specs=VMEM,
        compiler_params=params,
        name="pack",
    )(hub_list, in_hbm(feat), in_hbm(send_list))
    gathered = lax.all_gather(payload, "h", axis=0, tiled=True)
    outgoing = pl.pallas_call(
        select_kernel,
        out_shape=pltpu.HBM((NEAR, SENT, TILE), bf16),
        in_specs=[VMEM],
        out_specs=ANY,
        scratch_shapes=[
            pltpu.VMEM((H, TILE), jnp.int32),
            pltpu.SMEM((H, TILE), jnp.int32),
            pltpu.VMEM((NEAR, SENT, TILE), bf16),
            pltpu.SemaphoreType.DMA,
            pltpu.SemaphoreType.DMA((NEAR,)),
        ],
        compiler_params=params,
        cost_estimate=pl.CostEstimate(flops=0, bytes_accessed=6_000_000, transcendentals=0),
        name="select",
    )(gathered)
    outgoing, feat = lax.optimization_barrier((outgoing, feat))
    received = lax.all_to_all(outgoing, ("y", "l", "c"), split_axis=0, concat_axis=0, tiled=True)
    base, early = pl.pallas_call(
        fetch_kernel,
        out_shape=(pltpu.HBM((BLOCKS, TILE), f32), pltpu.VMEM((EARLY, TILE, TILE), bf16)),
        in_specs=[VMEM, VMEM, ANY],
        out_specs=(VMEM, ANY),
        scratch_shapes=[pltpu.SemaphoreType.DMA],
        compiler_params=params,
        cost_estimate=pl.CostEstimate(flops=8_400_000, bytes_accessed=3_000_000, transcendentals=0),
        name="fetch",
    )(in_hbm(feat), in_hbm(local_tiles), in_hbm(stripe_tiles))
    aggregated = pl.pallas_call(
        stripe_kernel,
        out_shape=pltpu.HBM((COL * W, ROWB * TILE), bf16),
        in_specs=[SMEM, SMEM, SMEM, SMEM, VMEM, VMEM, VMEM, ANY, ANY],
        out_specs=VMEM,
        scratch_shapes=[
            pltpu.VMEM((ROWB, 2, TILE, TILE), bf16),
            pltpu.VMEM((CAP - EARLY, TILE, TILE), bf16),
            pltpu.VMEM((ROWB + 1, TILE, W), f32),
            pltpu.SemaphoreType.DMA,
            pltpu.SemaphoreType.DMA((PARTS,)),
        ],
        compiler_params=params,
        name="stripes",
    )(
        hub_ref,
        stripe_slot,
        stripe_target,
        stripe_live,
        received.reshape(NEAR * SENT, TILE),
        in_hbm(base),
        in_vmem(early),
        in_hbm(hub_tiles),
        in_hbm(stripe_tiles),
    )
    full = lax.all_to_all(aggregated, "x", split_axis=0, concat_axis=0, tiled=True)
    weight_cols = lax.dynamic_slice_in_dim(weight, lax.axis_index("x") * W, W, 1)
    result = jnp.dot(weight_cols.T, full, preferred_element_type=f32)
    return result.astype(bf16).T


def solution(mesh):
    split = Mesh(mesh.devices.reshape(Y, H, L, C, COL), ("y", "h", "l", "c", "x"))
    node = ("y", "h", "l", "c")
    in_specs = (
        P(node, "x"),
        P(node, None, None),
        P(node, None, None, None),
        P(node, None),
        P(node),
        P(node, None),
        P(node, None, None),
        P(node, None),
        P(node, None),
        P(node),
        P(),
    )
    return jax.shard_map(local, mesh=split, in_specs=in_specs, out_specs=P(node, "x"), check_vma=False)
```

```python
import jax
import jax.numpy as jnp
from jax import lax
from jax.experimental import pallas as pl
from jax.experimental.pallas import tpu as pltpu
from jax.sharding import Mesh, PartitionSpec as P

Y, H, L, C, COL = 4, 8, 2, 2, 4
ROWB, TILE, W = 8, 128, 32
NEAR = Y * L
CAP = 128
EARLY = 96
BLOCKS = ROWB * W
PAY = BLOCKS + 16
SENT = (C + 1) * H * W
KEPT = 2 * H * W
NT = (((1,), (1,)), ((), ()))
VMEM = pl.BlockSpec(memory_space=pltpu.VMEM)
SMEM = pl.BlockSpec(memory_space=pltpu.SMEM)
ANY = pl.BlockSpec(memory_space=pl.ANY)


def rows_of(start):
    return pl.ds(pl.multiple_of(start, 16), W)


def in_hbm(array):
    return pltpu.with_memory_space_constraint(array, pltpu.HBM)


def in_vmem(array):
    return pltpu.with_memory_space_constraint(array, pltpu.VMEM)


def pack_kernel(hub_list, feat, send, out):
    for b in range(ROWB):
        out[b * W : (b + 1) * W, :] = feat[:, b * TILE : (b + 1) * TILE]
    row = lax.broadcasted_iota(jnp.int32, (16, TILE), 0)
    meta = jnp.where(row == 0, jnp.broadcast_to(send[...], (16, TILE)), hub_list[0])
    out[BLOCKS:PAY, :] = meta.astype(jnp.float32).astype(jnp.bfloat16)


def select_kernel(gathered, out, index_vmem, index, buffer, sem, sems):
    for h in range(H):
        meta = gathered[h * PAY + BLOCKS : (h + 1) * PAY, :].astype(jnp.float32)
        index_vmem[2 * h : 2 * h + 2, :] = meta[:2].astype(jnp.int32)
    copy = pltpu.make_async_copy(index_vmem, index, sem)
    copy.start()
    copy.wait()
    pair = lax.axis_index("h")
    hubs = [gathered[rows_of(h * PAY + index[2 * h + 1, 0] * W), :] for h in range(H)]
    copies = []
    for m in range(NEAR):
        for c in range(C):
            reader = (m // L) * (H * L * C) + pair * (L * C) + (m % L) * C + c
            for h in range(H):
                block = index[2 * h, reader]
                at = (c * H + h) * W
                buffer[m, at : at + W, :] = gathered[rows_of(h * PAY + block * W), :]
        for h in range(H):
            at = (C * H + h) * W
            buffer[m, at : at + W, :] = hubs[h]
        copies.append(pltpu.make_async_copy(buffer.at[m], out.at[m], sems.at[m]))
        copies[-1].start()
    for copy in copies:
        copy.wait()


def fetch_kernel(feat, local_tiles, tiles_hbm, out, tiles, sem):
    copy = pltpu.make_async_copy(tiles_hbm.at[pl.ds(0, EARLY)], tiles, sem)
    copy.start()
    for b in range(ROWB):
        out[b * W : (b + 1) * W, :] = lax.dot_general(
            feat[:, b * TILE : (b + 1) * TILE], local_tiles[b], NT, preferred_element_type=jnp.float32
        )
    copy.wait()


def stripe_kernel(
    hub_ref, slot, target, live, own, other, base, early, hub_hbm, tiles_hbm, out, blocks, hub_tiles, late, acc, sems
):
    core = lax.axis_index("c")
    half = H * W
    copies = []
    for k, (source, place) in enumerate(((own, core), (other, 1 - core))):
        for part in range(2):
            rows = pl.ds(core * half, half) if part == 0 else pl.ds(C * half, half)
            into = blocks.at[pl.ds(place * NEAR, NEAR), pl.ds(part * half, half)]
            copies.append(pltpu.make_async_copy(source.at[:, rows], into, sems.at[2 * k + part]))
    copies.append(pltpu.make_async_copy(tiles_hbm.at[pl.ds(EARLY, CAP - EARLY)], late, sems.at[4]))
    copies.append(pltpu.make_async_copy(hub_hbm, hub_tiles, sems.at[5]))
    for k in (0, 2, 1, 3, 4, 5):
        copies[k].start()

    def product(tile, node, first):
        near = (node & 1) * NEAR + lax.shift_right_logical(node, 5) * L + (lax.shift_right_logical(node, 1) & 1)
        rows = rows_of(first + (lax.shift_right_logical(node, 2) & 7) * W)
        return lax.dot_general(tile, blocks[near, rows, :], NT, preferred_element_type=jnp.float32)

    for b in range(ROWB + 1):
        acc[b] = jnp.zeros((TILE, W), jnp.float32)
    count = live[0]
    copies[0].wait()
    copies[2].wait()
    for s in range(CAP):
        if s == EARLY:
            copies[4].wait()
        tile = early[s] if s < EARLY else late[s - EARLY]
        row = jnp.where(s < count, target[0, s], ROWB)
        acc[row] += product(tile, slot[0, s], 0)
    for k in (1, 3, 5):
        copies[k].wait()
    for b in range(ROWB):
        total = acc[b]
        for j in range(2):
            total += product(hub_tiles[b, j], hub_ref[b, j], half)
        agg = (total.T + base[b * W : (b + 1) * W, :]).astype(jnp.bfloat16)
        for k in range(COL):
            out[k * W : (k + 1) * W, b * TILE : (b + 1) * TILE] = agg


def local(
    features,
    local_tiles,
    hub_tiles,
    hub_ref,
    hub_list,
    send_list,
    stripe_tiles,
    stripe_slot,
    stripe_target,
    stripe_live,
    weight,
):
    bf16, f32 = jnp.bfloat16, jnp.float32
    params = pltpu.CompilerParams(vmem_limit_bytes=16 * 1024 * 1024)
    feat = features.T
    payload = pl.pallas_call(
        pack_kernel,
        out_shape=jax.ShapeDtypeStruct((PAY, TILE), bf16),
        in_specs=[SMEM, VMEM, VMEM],
        out_specs=VMEM,
        compiler_params=params,
        name="pack",
    )(hub_list, in_hbm(feat), in_hbm(send_list))
    gathered = lax.all_gather(payload, "h", axis=0, tiled=True)
    outgoing = pl.pallas_call(
        select_kernel,
        out_shape=pltpu.HBM((NEAR, SENT, TILE), bf16),
        in_specs=[VMEM],
        out_specs=ANY,
        scratch_shapes=[
            pltpu.VMEM((2 * H, TILE), jnp.int32),
            pltpu.SMEM((2 * H, TILE), jnp.int32),
            pltpu.VMEM((NEAR, SENT, TILE), bf16),
            pltpu.SemaphoreType.DMA,
            pltpu.SemaphoreType.DMA((NEAR,)),
        ],
        compiler_params=params,
        cost_estimate=pl.CostEstimate(flops=0, bytes_accessed=6_000_000, transcendentals=0),
        name="select",
    )(gathered)
    outgoing, feat = lax.optimization_barrier((outgoing, feat))
    received = lax.all_to_all(outgoing, ("y", "l"), split_axis=0, concat_axis=0, tiled=True)
    base, early = pl.pallas_call(
        fetch_kernel,
        out_shape=(pltpu.HBM((BLOCKS, TILE), f32), pltpu.VMEM((EARLY, TILE, TILE), bf16)),
        in_specs=[VMEM, VMEM, ANY],
        out_specs=(VMEM, ANY),
        scratch_shapes=[pltpu.SemaphoreType.DMA],
        compiler_params=params,
        cost_estimate=pl.CostEstimate(flops=8_400_000, bytes_accessed=3_000_000, transcendentals=0),
        name="fetch",
    )(in_hbm(feat), in_hbm(local_tiles), in_hbm(stripe_tiles))
    received, early = lax.optimization_barrier((received, early))
    other = lax.ppermute(received, "c", [(0, 1), (1, 0)])
    aggregated = pl.pallas_call(
        stripe_kernel,
        out_shape=pltpu.HBM((COL * W, ROWB * TILE), bf16),
        in_specs=[SMEM, SMEM, SMEM, SMEM, ANY, ANY, VMEM, VMEM, ANY, ANY],
        out_specs=VMEM,
        scratch_shapes=[
            pltpu.VMEM((C * NEAR, KEPT, TILE), bf16),
            pltpu.VMEM((ROWB, 2, TILE, TILE), bf16),
            pltpu.VMEM((CAP - EARLY, TILE, TILE), bf16),
            pltpu.VMEM((ROWB + 1, TILE, W), f32),
            pltpu.SemaphoreType.DMA((6,)),
        ],
        compiler_params=params,
        name="stripes",
    )(
        hub_ref,
        stripe_slot,
        stripe_target,
        stripe_live,
        in_hbm(received),
        in_hbm(other),
        in_hbm(base),
        in_vmem(early),
        in_hbm(hub_tiles),
        in_hbm(stripe_tiles),
    )
    full = lax.all_to_all(aggregated, "x", split_axis=0, concat_axis=0, tiled=True)
    weight_cols = lax.dynamic_slice_in_dim(weight, lax.axis_index("x") * W, W, 1)
    result = jnp.dot(weight_cols.T, full, preferred_element_type=f32)
    return result.astype(bf16).T


def solution(mesh):
    split = Mesh(mesh.devices.reshape(Y, H, L, C, COL), ("y", "h", "l", "c", "x"))
    node = ("y", "h", "l", "c")
    in_specs = (
        P(node, "x"),
        P(node, None, None),
        P(node, None, None, None),
        P(node, None),
        P(node),
        P(node, None),
        P(node, None, None),
        P(node, None),
        P(node, None),
        P(node),
        P(),
    )
    return jax.shard_map(local, mesh=split, in_specs=in_specs, out_specs=P(node, "x"), check_vma=False)
```

```python
import jax
import jax.numpy as jnp
from jax import lax
from jax.experimental import pallas as pl
from jax.experimental.pallas import tpu as pltpu
from jax.sharding import Mesh, PartitionSpec as P

Y, H, L, C, COL = 4, 8, 2, 2, 4
ROWB, TILE, W = 8, 128, 32
NEAR = Y * L
CAP = 128
EARLY = 96
BLOCKS = ROWB * W
PAY = BLOCKS + 16
SENT = (C + 1) * H * W
KEPT = 2 * H * W
NT = (((1,), (1,)), ((), ()))
VMEM = pl.BlockSpec(memory_space=pltpu.VMEM)
SMEM = pl.BlockSpec(memory_space=pltpu.SMEM)
ANY = pl.BlockSpec(memory_space=pl.ANY)


def rows_of(start):
    return pl.ds(pl.multiple_of(start, 16), W)


def in_hbm(array):
    return pltpu.with_memory_space_constraint(array, pltpu.HBM)


def in_vmem(array):
    return pltpu.with_memory_space_constraint(array, pltpu.VMEM)


def pack_kernel(hub_list, feat, send, out):
    for b in range(ROWB):
        out[b * W : (b + 1) * W, :] = feat[:, b * TILE : (b + 1) * TILE]
    row = lax.broadcasted_iota(jnp.int32, (16, TILE), 0)
    meta = jnp.where(row == 0, jnp.broadcast_to(send[...], (16, TILE)), hub_list[0])
    out[BLOCKS:PAY, :] = meta.astype(jnp.float32).astype(jnp.bfloat16)


def select_kernel(gathered, out, index_vmem, index, buffer, sem, sems):
    for h in range(H):
        meta = gathered[h * PAY + BLOCKS : (h + 1) * PAY, :].astype(jnp.float32)
        index_vmem[2 * h : 2 * h + 2, :] = meta[:2].astype(jnp.int32)
    copy = pltpu.make_async_copy(index_vmem, index, sem)
    copy.start()
    copy.wait()
    pair = lax.axis_index("h")
    hubs = [gathered[rows_of(h * PAY + index[2 * h + 1, 0] * W), :] for h in range(H)]
    copies = []
    for m in range(NEAR):
        for c in range(C):
            reader = (m % Y) * (H * L * C) + pair * (L * C) + (m // Y) * C + c
            for h in range(H):
                block = index[2 * h, reader]
                at = (c * H + h) * W
                buffer[m, at : at + W, :] = gathered[rows_of(h * PAY + block * W), :]
        for h in range(H):
            at = (C * H + h) * W
            buffer[m, at : at + W, :] = hubs[h]
        copies.append(pltpu.make_async_copy(buffer.at[m], out.at[m], sems.at[m]))
        copies[-1].start()
    for copy in copies:
        copy.wait()


def fetch_kernel(feat, local_tiles, tiles_hbm, out, tiles, sem):
    copy = pltpu.make_async_copy(tiles_hbm.at[pl.ds(0, EARLY)], tiles, sem)
    copy.start()
    for b in range(ROWB):
        out[b * W : (b + 1) * W, :] = lax.dot_general(
            feat[:, b * TILE : (b + 1) * TILE], local_tiles[b], NT, preferred_element_type=jnp.float32
        )
    copy.wait()


def stripe_kernel(
    hub_ref, slot, target, live, own, other, base, early, hub_hbm, tiles_hbm, out, blocks, hub_tiles, late, acc, sems
):
    core = lax.axis_index("c")
    half = H * W
    copies = []
    for k, (source, place) in enumerate(((own, core), (other, 1 - core))):
        for part in range(2):
            rows = pl.ds(core * half, half) if part == 0 else pl.ds(C * half, half)
            into = blocks.at[pl.ds(place * NEAR, NEAR), pl.ds(part * half, half)]
            copies.append(pltpu.make_async_copy(source.at[:, rows], into, sems.at[2 * k + part]))
    copies.append(pltpu.make_async_copy(tiles_hbm.at[pl.ds(EARLY, CAP - EARLY)], late, sems.at[4]))
    copies.append(pltpu.make_async_copy(hub_hbm, hub_tiles, sems.at[5]))
    for k in (0, 2, 1, 3, 4, 5):
        copies[k].start()

    def product(tile, node, first):
        near = (node & 1) * NEAR + lax.shift_right_logical(node, 5) + (lax.shift_right_logical(node, 1) & 1) * Y
        rows = rows_of(first + (lax.shift_right_logical(node, 2) & 7) * W)
        return lax.dot_general(tile, blocks[near, rows, :], NT, preferred_element_type=jnp.float32)

    for b in range(ROWB + 1):
        acc[b] = jnp.zeros((TILE, W), jnp.float32)
    count = live[0]
    copies[0].wait()
    copies[2].wait()
    for s in range(CAP):
        if s == EARLY:
            copies[4].wait()
        tile = early[s] if s < EARLY else late[s - EARLY]
        row = jnp.where(s < count, target[0, s], ROWB)
        acc[row] += product(tile, slot[0, s], 0)
    for k in (1, 3, 5):
        copies[k].wait()
    for b in range(ROWB):
        total = acc[b]
        for j in range(2):
            total += product(hub_tiles[b, j], hub_ref[b, j], half)
        agg = (total.T + base[b * W : (b + 1) * W, :]).astype(jnp.bfloat16)
        for k in range(COL):
            out[k * W : (k + 1) * W, b * TILE : (b + 1) * TILE] = agg


def local(
    features,
    local_tiles,
    hub_tiles,
    hub_ref,
    hub_list,
    send_list,
    stripe_tiles,
    stripe_slot,
    stripe_target,
    stripe_live,
    weight,
):
    bf16, f32 = jnp.bfloat16, jnp.float32
    params = pltpu.CompilerParams(vmem_limit_bytes=16 * 1024 * 1024)
    feat = features.T
    payload = pl.pallas_call(
        pack_kernel,
        out_shape=jax.ShapeDtypeStruct((PAY, TILE), bf16),
        in_specs=[SMEM, VMEM, VMEM],
        out_specs=VMEM,
        compiler_params=params,
        name="pack",
    )(hub_list, in_hbm(feat), in_hbm(send_list))
    gathered = lax.all_gather(payload, "h", axis=0, tiled=True)
    outgoing = pl.pallas_call(
        select_kernel,
        out_shape=pltpu.HBM((NEAR, SENT, TILE), bf16),
        in_specs=[VMEM],
        out_specs=ANY,
        scratch_shapes=[
            pltpu.VMEM((2 * H, TILE), jnp.int32),
            pltpu.SMEM((2 * H, TILE), jnp.int32),
            pltpu.VMEM((NEAR, SENT, TILE), bf16),
            pltpu.SemaphoreType.DMA,
            pltpu.SemaphoreType.DMA((NEAR,)),
        ],
        compiler_params=params,
        cost_estimate=pl.CostEstimate(flops=0, bytes_accessed=6_000_000, transcendentals=0),
        name="select",
    )(gathered)
    outgoing, feat = lax.optimization_barrier((outgoing, feat))
    received = lax.all_to_all(outgoing, ("l", "y"), split_axis=0, concat_axis=0, tiled=True)
    base, early = pl.pallas_call(
        fetch_kernel,
        out_shape=(pltpu.HBM((BLOCKS, TILE), f32), pltpu.VMEM((EARLY, TILE, TILE), bf16)),
        in_specs=[VMEM, VMEM, ANY],
        out_specs=(VMEM, ANY),
        scratch_shapes=[pltpu.SemaphoreType.DMA],
        compiler_params=params,
        cost_estimate=pl.CostEstimate(flops=8_400_000, bytes_accessed=3_000_000, transcendentals=0),
        name="fetch",
    )(in_hbm(feat), in_hbm(local_tiles), in_hbm(stripe_tiles))
    received, early = lax.optimization_barrier((received, early))
    other = lax.ppermute(received, "c", [(0, 1), (1, 0)])
    aggregated = pl.pallas_call(
        stripe_kernel,
        out_shape=pltpu.HBM((COL * W, ROWB * TILE), bf16),
        in_specs=[SMEM, SMEM, SMEM, SMEM, ANY, ANY, VMEM, VMEM, ANY, ANY],
        out_specs=VMEM,
        scratch_shapes=[
            pltpu.VMEM((C * NEAR, KEPT, TILE), bf16),
            pltpu.VMEM((ROWB, 2, TILE, TILE), bf16),
            pltpu.VMEM((CAP - EARLY, TILE, TILE), bf16),
            pltpu.VMEM((ROWB + 1, TILE, W), f32),
            pltpu.SemaphoreType.DMA((6,)),
        ],
        compiler_params=params,
        name="stripes",
    )(
        hub_ref,
        stripe_slot,
        stripe_target,
        stripe_live,
        in_hbm(received),
        in_hbm(other),
        in_hbm(base),
        in_vmem(early),
        in_hbm(hub_tiles),
        in_hbm(stripe_tiles),
    )
    full = lax.all_to_all(aggregated, "x", split_axis=0, concat_axis=0, tiled=True)
    weight_cols = lax.dynamic_slice_in_dim(weight, lax.axis_index("x") * W, W, 1)
    result = jnp.dot(weight_cols.T, full, preferred_element_type=f32)
    return result.astype(bf16).T


def solution(mesh):
    split = Mesh(mesh.devices.reshape(Y, H, L, C, COL), ("y", "h", "l", "c", "x"))
    node = ("y", "h", "l", "c")
    in_specs = (
        P(node, "x"),
        P(node, None, None),
        P(node, None, None, None),
        P(node, None),
        P(node),
        P(node, None),
        P(node, None, None),
        P(node, None),
        P(node, None),
        P(node),
        P(),
    )
    return jax.shard_map(local, mesh=split, in_specs=in_specs, out_specs=P(node, "x"), check_vma=False)
```

```python
import jax
import jax.numpy as jnp
from jax import lax
from jax.experimental import pallas as pl
from jax.experimental.pallas import tpu as pltpu
from jax.sharding import Mesh, PartitionSpec as P

Y, H, L, C, COL = 4, 8, 2, 2, 4
ROWB, TILE, W = 8, 128, 32
NEAR = Y * L
CAP = 128
EARLY = 56
BLOCKS = ROWB * W
PAY = BLOCKS + 16
SENT = (C + 1) * H * W
KEPT = 2 * H * W
NT = (((1,), (1,)), ((), ()))
VMEM = pl.BlockSpec(memory_space=pltpu.VMEM)
SMEM = pl.BlockSpec(memory_space=pltpu.SMEM)
ANY = pl.BlockSpec(memory_space=pl.ANY)


def rows_of(start):
    return pl.ds(pl.multiple_of(start, 16), W)


def in_hbm(array):
    return pltpu.with_memory_space_constraint(array, pltpu.HBM)


def in_vmem(array):
    return pltpu.with_memory_space_constraint(array, pltpu.VMEM)


def pack_kernel(hub_list, feat, send, out):
    for b in range(ROWB):
        out[b * W : (b + 1) * W, :] = feat[:, b * TILE : (b + 1) * TILE]
    row = lax.broadcasted_iota(jnp.int32, (16, TILE), 0)
    meta = jnp.where(row == 0, jnp.broadcast_to(send[...], (16, TILE)), hub_list[0])
    out[BLOCKS:PAY, :] = meta.astype(jnp.float32).astype(jnp.bfloat16)


def select_kernel(gathered, out, index_vmem, index, buffer, sem, sems):
    for h in range(H):
        meta = gathered[h * PAY + BLOCKS : (h + 1) * PAY, :].astype(jnp.float32)
        index_vmem[2 * h : 2 * h + 2, :] = meta[:2].astype(jnp.int32)
    copy = pltpu.make_async_copy(index_vmem, index, sem)
    copy.start()
    copy.wait()
    pair = lax.axis_index("h")
    hubs = [gathered[rows_of(h * PAY + index[2 * h + 1, 0] * W), :] for h in range(H)]
    copies = []
    for m in range(NEAR):
        for c in range(C):
            reader = (m % Y) * (H * L * C) + pair * (L * C) + (m // Y) * C + c
            for h in range(H):
                block = index[2 * h, reader]
                at = (c * H + h) * W
                buffer[m, at : at + W, :] = gathered[rows_of(h * PAY + block * W), :]
        for h in range(H):
            at = (C * H + h) * W
            buffer[m, at : at + W, :] = hubs[h]
        copies.append(pltpu.make_async_copy(buffer.at[m], out.at[m], sems.at[m]))
        copies[-1].start()
    for copy in copies:
        copy.wait()


def fetch_kernel(feat, local_tiles, tiles_hbm, out, tiles, sem):
    copy = pltpu.make_async_copy(tiles_hbm.at[pl.ds(0, EARLY)], tiles, sem)
    copy.start()
    for b in range(ROWB):
        out[b * W : (b + 1) * W, :] = lax.dot_general(
            feat[:, b * TILE : (b + 1) * TILE], local_tiles[b], NT, preferred_element_type=jnp.float32
        )
    copy.wait()


def stripe_kernel(
    hub_ref, slot, target, live, own, other, base, early, hub_hbm, tiles_hbm, out, blocks, hub_tiles, late, acc, sems
):
    core = lax.axis_index("c")
    half = H * W
    copies = []
    for k, (source, place) in enumerate(((own, core), (other, 1 - core))):
        for part in range(2):
            rows = pl.ds(core * half, half) if part == 0 else pl.ds(C * half, half)
            into = blocks.at[pl.ds(place * NEAR, NEAR), pl.ds(part * half, half)]
            copies.append(pltpu.make_async_copy(source.at[:, rows], into, sems.at[2 * k + part]))
    copies.append(pltpu.make_async_copy(tiles_hbm.at[pl.ds(EARLY, CAP - EARLY)], late, sems.at[4]))
    copies.append(pltpu.make_async_copy(hub_hbm, hub_tiles, sems.at[5]))
    for k in (0, 2, 1, 3, 4, 5):
        copies[k].start()

    def product(tile, node, first):
        near = (node & 1) * NEAR + lax.shift_right_logical(node, 5) + (lax.shift_right_logical(node, 1) & 1) * Y
        rows = rows_of(first + (lax.shift_right_logical(node, 2) & 7) * W)
        return lax.dot_general(tile, blocks[near, rows, :], NT, preferred_element_type=jnp.float32)

    for b in range(ROWB + 1):
        acc[b] = jnp.zeros((TILE, W), jnp.float32)
    count = live[0]
    copies[0].wait()
    copies[2].wait()
    for s in range(CAP):
        if s == EARLY:
            copies[4].wait()
        tile = early[s] if s < EARLY else late[s - EARLY]
        row = jnp.where(s < count, target[0, s], ROWB)
        acc[row] += product(tile, slot[0, s], 0)
    for k in (1, 3, 5):
        copies[k].wait()
    for b in range(ROWB):
        total = acc[b]
        for j in range(2):
            total += product(hub_tiles[b, j], hub_ref[b, j], half)
        agg = (total.T + base[b * W : (b + 1) * W, :]).astype(jnp.bfloat16)
        for k in range(COL):
            out[k * W : (k + 1) * W, b * TILE : (b + 1) * TILE] = agg


def local(
    features,
    local_tiles,
    hub_tiles,
    hub_ref,
    hub_list,
    send_list,
    stripe_tiles,
    stripe_slot,
    stripe_target,
    stripe_live,
    weight,
):
    bf16, f32 = jnp.bfloat16, jnp.float32
    params = pltpu.CompilerParams(vmem_limit_bytes=16 * 1024 * 1024)
    feat = features.T
    payload = pl.pallas_call(
        pack_kernel,
        out_shape=jax.ShapeDtypeStruct((PAY, TILE), bf16),
        in_specs=[SMEM, VMEM, VMEM],
        out_specs=VMEM,
        compiler_params=params,
        name="pack",
    )(hub_list, in_hbm(feat), in_hbm(send_list))
    gathered = lax.all_gather(payload, "h", axis=0, tiled=True)
    outgoing = pl.pallas_call(
        select_kernel,
        out_shape=pltpu.HBM((NEAR, SENT, TILE), bf16),
        in_specs=[VMEM],
        out_specs=ANY,
        scratch_shapes=[
            pltpu.VMEM((2 * H, TILE), jnp.int32),
            pltpu.SMEM((2 * H, TILE), jnp.int32),
            pltpu.VMEM((NEAR, SENT, TILE), bf16),
            pltpu.SemaphoreType.DMA,
            pltpu.SemaphoreType.DMA((NEAR,)),
        ],
        compiler_params=params,
        cost_estimate=pl.CostEstimate(flops=0, bytes_accessed=6_000_000, transcendentals=0),
        name="select",
    )(gathered)
    outgoing, feat = lax.optimization_barrier((outgoing, feat))
    received = lax.all_to_all(outgoing, ("l", "y"), split_axis=0, concat_axis=0, tiled=True)
    base, early = pl.pallas_call(
        fetch_kernel,
        out_shape=(pltpu.HBM((BLOCKS, TILE), f32), pltpu.VMEM((EARLY, TILE, TILE), bf16)),
        in_specs=[VMEM, VMEM, ANY],
        out_specs=(VMEM, ANY),
        scratch_shapes=[pltpu.SemaphoreType.DMA],
        compiler_params=params,
        cost_estimate=pl.CostEstimate(flops=8_400_000, bytes_accessed=3_000_000, transcendentals=0),
        name="fetch",
    )(in_hbm(feat), in_hbm(local_tiles), in_hbm(stripe_tiles))
    received, early = lax.optimization_barrier((received, early))
    other = lax.ppermute(received, "c", [(0, 1), (1, 0)])
    aggregated = pl.pallas_call(
        stripe_kernel,
        out_shape=pltpu.HBM((COL * W, ROWB * TILE), bf16),
        in_specs=[SMEM, SMEM, SMEM, SMEM, ANY, ANY, VMEM, VMEM, ANY, ANY],
        out_specs=VMEM,
        scratch_shapes=[
            pltpu.VMEM((C * NEAR, KEPT, TILE), bf16),
            pltpu.VMEM((ROWB, 2, TILE, TILE), bf16),
            pltpu.VMEM((CAP - EARLY, TILE, TILE), bf16),
            pltpu.VMEM((ROWB + 1, TILE, W), f32),
            pltpu.SemaphoreType.DMA((6,)),
        ],
        compiler_params=params,
        name="stripes",
    )(
        hub_ref,
        stripe_slot,
        stripe_target,
        stripe_live,
        received,
        in_hbm(other),
        in_hbm(base),
        in_vmem(early),
        in_hbm(hub_tiles),
        in_hbm(stripe_tiles),
    )
    full = lax.all_to_all(aggregated, "x", split_axis=0, concat_axis=0, tiled=True)
    weight_cols = lax.dynamic_slice_in_dim(weight, lax.axis_index("x") * W, W, 1)
    result = jnp.dot(weight_cols.T, full, preferred_element_type=f32)
    return result.astype(bf16).T


def solution(mesh):
    split = Mesh(mesh.devices.reshape(Y, H, L, C, COL), ("y", "h", "l", "c", "x"))
    node = ("y", "h", "l", "c")
    in_specs = (
        P(node, "x"),
        P(node, None, None),
        P(node, None, None, None),
        P(node, None),
        P(node),
        P(node, None),
        P(node, None, None),
        P(node, None),
        P(node, None),
        P(node),
        P(),
    )
    return jax.shard_map(local, mesh=split, in_specs=in_specs, out_specs=P(node, "x"), check_vma=False)
```

```python
import jax
import jax.numpy as jnp
from jax import lax
from jax.experimental import pallas as pl
from jax.experimental.pallas import tpu as pltpu
from jax.sharding import Mesh, PartitionSpec as P

Y, H, L, C, COL = 4, 8, 2, 2, 4
ROWB, TILE, W = 8, 128, 32
NEAR = Y * L
CAP = 128
EARLY = 104
BLOCKS = ROWB * W
PAY = BLOCKS + 16
SENT = (C + 1) * H * W
KEPT = 2 * H * W
NT = (((1,), (1,)), ((), ()))
VMEM = pl.BlockSpec(memory_space=pltpu.VMEM)
SMEM = pl.BlockSpec(memory_space=pltpu.SMEM)
ANY = pl.BlockSpec(memory_space=pl.ANY)


def rows_of(start):
    return pl.ds(pl.multiple_of(start, 16), W)


def in_hbm(array):
    return pltpu.with_memory_space_constraint(array, pltpu.HBM)


def in_vmem(array):
    return pltpu.with_memory_space_constraint(array, pltpu.VMEM)


def pack_kernel(hub_list, feat, send, out):
    for b in range(ROWB):
        out[b * W : (b + 1) * W, :] = feat[:, b * TILE : (b + 1) * TILE]
    row = lax.broadcasted_iota(jnp.int32, (16, TILE), 0)
    meta = jnp.where(row == 0, jnp.broadcast_to(send[...], (16, TILE)), hub_list[0])
    out[BLOCKS:PAY, :] = meta.astype(jnp.float32).astype(jnp.bfloat16)


def select_kernel(gathered, out, index_vmem, index, buffer, sem, sems):
    for h in range(H):
        meta = gathered[h * PAY + BLOCKS : (h + 1) * PAY, :].astype(jnp.float32)
        index_vmem[2 * h : 2 * h + 2, :] = meta[:2].astype(jnp.int32)
    copy = pltpu.make_async_copy(index_vmem, index, sem)
    copy.start()
    copy.wait()
    pair = lax.axis_index("h")
    hubs = [gathered[rows_of(h * PAY + index[2 * h + 1, 0] * W), :] for h in range(H)]
    copies = []
    for m in range(NEAR):
        for c in range(C):
            reader = (m % Y) * (H * L * C) + pair * (L * C) + (m // Y) * C + c
            for h in range(H):
                block = index[2 * h, reader]
                at = (c * H + h) * W
                buffer[m, at : at + W, :] = gathered[rows_of(h * PAY + block * W), :]
        for h in range(H):
            at = (C * H + h) * W
            buffer[m, at : at + W, :] = hubs[h]
        copies.append(pltpu.make_async_copy(buffer.at[m], out.at[m], sems.at[m]))
        copies[-1].start()
    for copy in copies:
        copy.wait()


def fetch_kernel(feat, local_tiles, tiles_hbm, out, tiles, sem):
    copy = pltpu.make_async_copy(tiles_hbm.at[pl.ds(0, EARLY)], tiles, sem)
    copy.start()
    for b in range(ROWB):
        out[b * W : (b + 1) * W, :] = lax.dot_general(
            feat[:, b * TILE : (b + 1) * TILE], local_tiles[b], NT, preferred_element_type=jnp.float32
        )
    copy.wait()


def stripe_kernel(
    hub_ref, slot, target, live, own, other, base, early, hub_hbm, tiles_hbm, out, blocks, hub_tiles, late, acc, sems
):
    core = lax.axis_index("c")
    half = H * W
    copies = []
    for k, (source, place) in enumerate(((own, core), (other, 1 - core))):
        for part in range(2):
            rows = pl.ds(core * half, half) if part == 0 else pl.ds(C * half, half)
            into = blocks.at[pl.ds(place * NEAR, NEAR), pl.ds(part * half, half)]
            copies.append(pltpu.make_async_copy(source.at[:, rows], into, sems.at[2 * k + part]))
    copies.append(pltpu.make_async_copy(tiles_hbm.at[pl.ds(EARLY, CAP - EARLY)], late, sems.at[4]))
    copies.append(pltpu.make_async_copy(hub_hbm, hub_tiles, sems.at[5]))
    for k in (0, 2, 1, 3, 4, 5):
        copies[k].start()

    def product(tile, node, first):
        near = (node & 1) * NEAR + lax.shift_right_logical(node, 5) + (lax.shift_right_logical(node, 1) & 1) * Y
        rows = rows_of(first + (lax.shift_right_logical(node, 2) & 7) * W)
        return lax.dot_general(tile, blocks[near, rows, :], NT, preferred_element_type=jnp.float32)

    for b in range(ROWB + 1):
        acc[b] = jnp.zeros((TILE, W), jnp.float32)
    count = live[0]
    copies[0].wait()
    copies[2].wait()
    for s in range(CAP):
        if s == EARLY:
            copies[4].wait()
        tile = early[s] if s < EARLY else late[s - EARLY]
        row = jnp.where(s < count, target[0, s], ROWB)
        acc[row] += product(tile, slot[0, s], 0)
    for k in (1, 3, 5):
        copies[k].wait()
    for b in range(ROWB):
        total = acc[b]
        for j in range(2):
            total += product(hub_tiles[b, j], hub_ref[b, j], half)
        agg = (total.T + base[b * W : (b + 1) * W, :]).astype(jnp.bfloat16)
        for k in range(COL):
            out[k * W : (k + 1) * W, b * TILE : (b + 1) * TILE] = agg


def local(
    features,
    local_tiles,
    hub_tiles,
    hub_ref,
    hub_list,
    send_list,
    stripe_tiles,
    stripe_slot,
    stripe_target,
    stripe_live,
    weight,
):
    bf16, f32 = jnp.bfloat16, jnp.float32
    params = pltpu.CompilerParams(vmem_limit_bytes=16 * 1024 * 1024)
    feat = features.T
    payload = pl.pallas_call(
        pack_kernel,
        out_shape=jax.ShapeDtypeStruct((PAY, TILE), bf16),
        in_specs=[SMEM, VMEM, VMEM],
        out_specs=VMEM,
        compiler_params=params,
        name="pack",
    )(hub_list, in_hbm(feat), in_hbm(send_list))
    gathered = lax.all_gather(payload, "h", axis=0, tiled=True)
    outgoing = pl.pallas_call(
        select_kernel,
        out_shape=pltpu.HBM((NEAR, SENT, TILE), bf16),
        in_specs=[VMEM],
        out_specs=ANY,
        scratch_shapes=[
            pltpu.VMEM((2 * H, TILE), jnp.int32),
            pltpu.SMEM((2 * H, TILE), jnp.int32),
            pltpu.VMEM((NEAR, SENT, TILE), bf16),
            pltpu.SemaphoreType.DMA,
            pltpu.SemaphoreType.DMA((NEAR,)),
        ],
        compiler_params=params,
        cost_estimate=pl.CostEstimate(flops=0, bytes_accessed=6_000_000, transcendentals=0),
        name="select",
    )(gathered)
    outgoing, feat = lax.optimization_barrier((outgoing, feat))
    received = lax.all_to_all(outgoing, ("l", "y"), split_axis=0, concat_axis=0, tiled=True)
    base, early = pl.pallas_call(
        fetch_kernel,
        out_shape=(pltpu.HBM((BLOCKS, TILE), f32), pltpu.VMEM((EARLY, TILE, TILE), bf16)),
        in_specs=[VMEM, VMEM, ANY],
        out_specs=(VMEM, ANY),
        scratch_shapes=[pltpu.SemaphoreType.DMA],
        compiler_params=params,
        cost_estimate=pl.CostEstimate(flops=8_400_000, bytes_accessed=3_000_000, transcendentals=0),
        name="fetch",
    )(in_hbm(feat), in_hbm(local_tiles), in_hbm(stripe_tiles))
    received, early = lax.optimization_barrier((received, early))
    other = lax.ppermute(received, "c", [(0, 1), (1, 0)])
    aggregated = pl.pallas_call(
        stripe_kernel,
        out_shape=pltpu.HBM((COL * W, ROWB * TILE), bf16),
        in_specs=[SMEM, SMEM, SMEM, SMEM, ANY, ANY, VMEM, VMEM, ANY, ANY],
        out_specs=VMEM,
        scratch_shapes=[
            pltpu.VMEM((C * NEAR, KEPT, TILE), bf16),
            pltpu.VMEM((ROWB, 2, TILE, TILE), bf16),
            pltpu.VMEM((CAP - EARLY, TILE, TILE), bf16),
            pltpu.VMEM((ROWB + 1, TILE, W), f32),
            pltpu.SemaphoreType.DMA((6,)),
        ],
        compiler_params=params,
        name="stripes",
    )(
        hub_ref,
        stripe_slot,
        stripe_target,
        stripe_live,
        in_hbm(received),
        in_hbm(other),
        in_hbm(base),
        in_vmem(early),
        in_hbm(hub_tiles),
        in_hbm(stripe_tiles),
    )
    full = lax.all_to_all(aggregated, "x", split_axis=0, concat_axis=0, tiled=True)
    weight_cols = lax.dynamic_slice_in_dim(weight, lax.axis_index("x") * W, W, 1)
    result = jnp.dot(weight_cols.T, full, preferred_element_type=f32)
    return result.astype(bf16).T


def solution(mesh):
    split = Mesh(mesh.devices.reshape(Y, H, L, C, COL), ("y", "h", "l", "c", "x"))
    node = ("y", "h", "l", "c")
    in_specs = (
        P(node, "x"),
        P(node, None, None),
        P(node, None, None, None),
        P(node, None),
        P(node),
        P(node, None),
        P(node, None, None),
        P(node, None),
        P(node, None),
        P(node),
        P(),
    )
    return jax.shard_map(local, mesh=split, in_specs=in_specs, out_specs=P(node, "x"), check_vma=False)
```
